128 devices in a mesh: gx: 4 (over x_hi, core), gy: 8 (over y, x_lo), gz: 4 (over z).
Axes of the slice: x: 4 (x_hi: 2, x_lo: 2; x = x_hi * 2 + x_lo), y: 4, z: 4, core: 2. Of those that a mesh axis runs over, the one named last changes fastest.
Arguments:
- partial_sums: float32 [128, 256, 4096], P(('gx', 'gy', 'gz')), may hold values from -448 to 448
- correction_pieces: float32 [128, 256, 4096], P(('gx', 'gy', 'gz')), may hold values from -60 to 60
- counts: float32 [128, 256, 4096], P(('gx', 'gy', 'gz')), may hold values from 0 to 3, as said below
Outputs:
- pixel_mean_grid: float32 [256, 4096], P('gz')
- preview: float32 [64, 1024], replicated
The draws below stay inside these ranges and needn't reach their ends.
Inputs may be any that keep to these rules, and one draw needn't show every extreme that they name: `counts`: weights are real-valued and nonnegative.
All inputs are finite; a program needn't handle non-finite values.
Results may differ from the reference program's by a relative error of at most 0.00002.
Values sent between devices are 32-bit elements; how exact they have to be, the bound alone decides.
No kernel may reach another device: no remote copies, remote signals or barrier semaphores. Data moves between devices by JAX's collectives and lax.ppermute only.
A program may use at most 128 MiB of HBM per device.

```python
import jax
import jax.numpy as jnp

WIDTH = 4096
ROWS = 256
POINT_PIECES = 128


def draw_counts(key, part):
    shard_pos = jnp.arange(POINT_PIECES, dtype=jnp.float32) / POINT_PIECES
    unit = jax.random.uniform(key, (POINT_PIECES, ROWS, WIDTH), dtype=jnp.float32)
    upper = 1.0 + 2.0 * shard_pos
    weights = upper[:, None, None] * unit
    return jnp.clip(weights, 0.0, 3.0).astype(jnp.float32)


def strengthened(drawn, own_key, source, target, parts, factor):
    owner, partner = [(jnp.arange(drawn.shape[position]) // (drawn.shape[position] // parts)).reshape([-1 if axis == position else 1 for axis in range(drawn.ndim)]) for position in (source, target)]
    chosen = jax.random.permutation(own_key, parts)[partner]
    strong = (owner == chosen) | (owner == (partner + parts // 2) % parts)
    return jnp.where(strong, factor * drawn, drawn)


def steps_of(rng, shape, cuts, low, high):
    loudness, own = 1.0, jax.random.fold_in(rng, 6)
    for dim, shards_of in cuts:
        draws = jnp.exp(jax.random.uniform(jax.random.fold_in(own, dim), (shards_of,), jnp.float32, low / len(cuts), high / len(cuts)))
        loudness = loudness * jnp.repeat(draws, shape[dim] // shards_of).reshape([-1 if axis == dim else 1 for axis in range(len(shape))])
    return loudness


def normal_values(own_key, shape, width, most, shards=(), held_as=jnp.bfloat16):
    drawn = width * jax.random.normal(own_key, shape, jnp.float32)
    if shards:
        drawn = drawn * steps_of(own_key, shape, shards, -0.22, 0.18)
    return jnp.clip(drawn, -most, most).astype(held_as)


def noise_with(own_key, dims, spread, reach, cuts, heavy, held_as=jnp.bfloat16):
    result = spread * jax.random.normal(own_key, dims, jnp.float32)
    if cuts:
        result = result * steps_of(own_key, dims, cuts, -0.22, 0.18)
    return jnp.clip(strengthened(result, jax.random.fold_in(own_key, 3), *heavy), -reach, reach).astype(held_as)


def setup_inputs(seed: int = 0) -> dict:
    splits = jax.random.split(jax.random.key(seed), 4)
    return {
        "partial_sums": noise_with(splits[0], (POINT_PIECES, ROWS, WIDTH), 20.0, 448.0, ((0, 128),), (0, 1, 128, 5.5), jnp.float32),
        "correction_pieces": normal_values(splits[1], (POINT_PIECES, ROWS, WIDTH), 10.0, 60.0, ((0, 128),), jnp.float32),
        "counts": draw_counts(jax.random.fold_in(splits[3], 71), 0),
    }


def reference(partial_sums, correction_pieces, counts):
    total = jnp.sum(partial_sums, axis=0) + jnp.sum(correction_pieces, axis=0)
    total_count = jnp.sum(counts, axis=0)
    pixel_mean_grid = total / (total_count + 1.0)
    blocks = pixel_mean_grid.reshape(ROWS // 4, 4, WIDTH // 4, 4)
    preview = jnp.mean(blocks, axis=(1, 3))
    return pixel_mean_grid, preview
```

```python
import functools

import jax
import jax.numpy as jnp
import numpy as np
from jax import lax
from jax.experimental import pallas as pl
from jax.experimental.pallas import tpu as pltpu
from jax.sharding import PartitionSpec as P

AXES = ("gx", "gy", "gz")
F32 = jnp.float32
VMEM_LIMIT = 48 * 1024 * 1024


def _coords(d):
    gx, gy, gz = d // 32, (d // 4) % 8, d % 4
    return (gx // 2) * 2 + gy % 2, gy // 2, gz, gx % 2


def _device(x, y, z, core):
    return ((x // 2) * 2 + core) * 32 + (y * 2 + x % 2) * 4 + z


def _shift(axis0, axis1, k):
    pairs = []
    for d in range(128):
        at = list(_coords(d))
        axis = (axis0, axis1)[at[3]]
        at[axis] = (at[axis] + k) % 4
        pairs.append((d, _device(*at)))
    return pairs


_SIBLING = [(d, d ^ 32) for d in range(128)]
X, Y, Z = 0, 1, 2


def _send(array, pairs):
    return lax.ppermute(array, AXES, pairs)


def _exchange(arrays, axis0, axis1):
    got = {k: _send(arrays[k], _shift(axis0, axis1, k)) for k in (2, 1, 3)}
    return [arrays[0], got[1], got[2], got[3]]


def _position():
    gx, gy, gz = (lax.axis_index(a) for a in AXES)
    core = gx % 2
    x, y = (gx // 2) * 2 + gy % 2, gy // 2
    first, second = jnp.where(core == 0, gz, y), jnp.where(core == 0, y, gz)
    return jnp.stack([core, first, second, x]).astype(jnp.int32)


def _tile(core, a, b):
    return jnp.where(core == 0, a * 8 + b, b * 8 + 4 + a)


def _split_kernel(pos, p, c, n, out):
    out[0, 0] = p[0] + c[0]
    out[1, 0] = n[0]


def _split(pos, p, c, n, k, own):
    def rows(b, pos):
        me = pos[0]
        core = me if own else 1 - me
        y, z = jnp.where(me == 0, pos[2], pos[1]), jnp.where(me == 0, pos[1], pos[2])
        a = (jnp.where(core == 0, z, y) + k) % 4
        return (0, _tile(core, a, b), 0)

    return rows


def _shape(*dims):
    return jax.ShapeDtypeStruct(dims, F32)


def _params():
    return pltpu.CompilerParams(vmem_limit_bytes=VMEM_LIMIT)


def _for_sibling(pos, p, c, n, k):
    rows = pl.BlockSpec((1, 8, 4096), _split(pos, p, c, n, k, False))
    return pl.pallas_call(
        _split_kernel,
        grid_spec=pltpu.PrefetchScalarGridSpec(
            num_scalar_prefetch=1,
            grid=(4,),
            in_specs=[rows, rows, rows],
            out_specs=pl.BlockSpec((2, 1, 8, 4096), lambda b, pos: (0, b, 0, 0)),
        ),
        out_shape=_shape(2, 4, 8, 4096),
        compiler_params=_params(),
        name="for_sibling",
    )(pos, p, c, n)


def _pair_kernel(pos, p, c, n, got, out):
    out[0, 0] = (p[0] + c[0]) + got[0, 0]
    out[1, 0] = n[0] + got[1, 0]


def _pair(pos, p, c, n, got, k):
    rows = pl.BlockSpec((1, 8, 4096), _split(pos, p, c, n, k, True))
    both = pl.BlockSpec((2, 1, 8, 4096), lambda b, pos: (0, b, 0, 0))
    return pl.pallas_call(
        _pair_kernel,
        grid_spec=pltpu.PrefetchScalarGridSpec(
            num_scalar_prefetch=1,
            grid=(4,),
            in_specs=[rows, rows, rows, both],
            out_specs=both,
        ),
        out_shape=_shape(2, 4, 8, 4096),
        compiler_params=_params(),
        name="pair_sum",
    )(pos, p, c, n, got)


def _second_kernel(pos, a, b, c, d, *outs):
    for k in range(4):
        i = (pos[2] + k) % 4
        outs[k][0] = (a[0, i] + b[0, i]) + (c[0, i] + d[0, i])


def _second(pos, parts):
    whole = pl.BlockSpec((1, 4, 8, 4096), lambda i, pos: (i, 0, 0, 0))
    one = pl.BlockSpec((1, 8, 4096), lambda i, pos: (i, 0, 0))
    return pl.pallas_call(
        _second_kernel,
        grid_spec=pltpu.PrefetchScalarGridSpec(
            num_scalar_prefetch=1, grid=(2,), in_specs=[whole] * 4, out_specs=[one] * 4
        ),
        out_shape=[_shape(2, 8, 4096)] * 4,
        compiler_params=_params(),
        name="first_axis_sum",
    )(pos, *parts)


def _third_kernel(pos, a, b, c, d, *outs):
    for k in range(4):
        at = pl.ds(pl.multiple_of(((pos[3] + k) % 4) * 1024, 1024), 1024)
        outs[k][...] = (a[:, :, at] + b[:, :, at]) + (c[:, :, at] + d[:, :, at])


def _third(pos, parts):
    return pl.pallas_call(
        _third_kernel,
        grid_spec=pltpu.PrefetchScalarGridSpec(num_scalar_prefetch=1, grid=(1,),
            in_specs=[pl.BlockSpec((2, 8, 4096), lambda i, pos: (0, 0, 0))] * 4,
            out_specs=[pl.BlockSpec((2, 8, 1024), lambda i, pos: (0, 0, 0))] * 4),
        out_shape=[_shape(2, 8, 1024)] * 4,
        compiler_params=_params(),
        name="second_axis_sum",
    )(pos, *parts)


def _mean_kernel(a, b, c, d, mean, preview):
    both = (a[...] + b[...]) + (c[...] + d[...])
    grid = both[0] / (both[1] + 1.0)
    mean[...] = grid
    four = jnp.concatenate(
        [jnp.sum(grid[0:4], axis=0, keepdims=True), jnp.sum(grid[4:8], axis=0, keepdims=True)], axis=0
    )
    for j in range(2):
        row = lax.broadcasted_iota(jnp.int32, (512, 128), 0)
        column = lax.broadcasted_iota(jnp.int32, (512, 128), 1)
        pool = jnp.where(row // 4 == column, 0.0625, 0.0).astype(F32)
        preview[:, j * 128 : (j + 1) * 128] = jnp.dot(
            four[:, j * 512 : (j + 1) * 512], pool, precision=lax.Precision.HIGHEST, preferred_element_type=F32
        )


def _mean(parts):
    return pl.pallas_call(
        _mean_kernel,
        out_shape=[_shape(8, 1024), _shape(2, 256)],
        compiler_params=_params(),
        name="mean_and_preview",
    )(*parts)


def _pack_kernel(mean, a, b, c, d, out):
    out[:, :1024] = mean[...]
    for k, part in enumerate((a, b, c, d)):
        out[2 * k : 2 * k + 2, 1024:] = part[...]


def _pack(mean, previews):
    return pl.pallas_call(_pack_kernel, out_shape=_shape(8, 1280), compiler_params=_params(), name="pack")(mean, *previews)


def _row_kernel(a, b, c, d, out):
    for k, part in enumerate((a, b, c, d)):
        out[k] = part[...]


def _row(parts):
    return pl.pallas_call(_row_kernel, out_shape=_shape(4, 8, 1280), compiler_params=_params(), name="gathered_row")(*parts)


def _final_kernel(pos, *refs):
    own, other, grid, preview, lines = refs[:4], refs[4:8], refs[8], refs[9], refs[10]
    core, x = pos[0], pos[3]
    y = jnp.where(core == 0, pos[2], pos[1])
    z = jnp.where(core == 0, pos[1], pos[2])
    for mine, parts in ((True, own), (False, other)):
        c = core if mine else 1 - core
        for k2 in range(4):
            for k1 in range(4):
                fy = (y - jnp.where(c == 0, k1, k2)) % 4
                fx = (x - jnp.where(c == 0, k2, k1)) % 4
                rows = pl.multiple_of((c * 4 + fy) * 8, 8)
                columns = pl.multiple_of(fx * 1024, 1024)
                grid[pl.ds(rows, 8), pl.ds(columns, 1024)] = parts[k2][k1, :, :1024]
                for k in range(4):
                    at = pl.ds(pl.multiple_of(fx * 256, 256), 256)
                    lines[(((z - k) % 4) * 2 + c) * 4 + fy, :, at] = parts[k2][k1, 2 * k : 2 * k + 2, 1024:]
    for i in range(8):
        preview[8 * i : 8 * i + 8, :] = jnp.concatenate([lines[4 * i + j] for j in range(4)], axis=0)


def _final(pos, own, other):
    return pl.pallas_call(
        _final_kernel,
        in_specs=[pl.BlockSpec(memory_space=pltpu.SMEM)] + [pl.BlockSpec()] * 8,
        out_shape=[_shape(64, 4096), _shape(64, 1024)],
        scratch_shapes=[pltpu.VMEM((32, 2, 1024), F32)],
        compiler_params=_params(),
        name="assemble",
    )(pos, *own, *other)


def _local(p, c, n):
    pos = _position()
    blocks = [None] * 4
    for k in (2, 1, 3, 0):
        got = _send(_for_sibling(pos, p, c, n, k), _SIBLING)
        blocks[k] = _pair(pos, p, c, n, got, k)
    parts = _exchange(blocks, Z, Y)
    parts = _exchange(_second(pos, parts), Y, Z)
    parts = _exchange(_third(pos, parts), X, X)
    mean, preview = _mean(parts)
    packed = _pack(mean, _exchange([preview] * 4, Z, Z))
    row = _row(_exchange([packed] * 4, Y, X))
    own = _exchange([row] * 4, X, Y)
    other = [_send(part, _SIBLING) for part in own]
    return _final(pos, own, other)


def solution(mesh):
    return jax.shard_map(
        _local,
        mesh=mesh,
        in_specs=(P(AXES, None, None),) * 3,
        out_specs=(P("gz", None), P(None, None)),
        check_vma=False,
    )
```

```python
import functools

import jax
import jax.numpy as jnp
import numpy as np
from jax import lax
from jax.experimental import pallas as pl
from jax.experimental.pallas import tpu as pltpu
from jax.sharding import PartitionSpec as P

AXES = ("gx", "gy", "gz")
F32 = jnp.float32
VMEM_LIMIT = 48 * 1024 * 1024


def _coords(d):
    gx, gy, gz = d // 32, (d // 4) % 8, d % 4
    return (gx // 2) * 2 + gy % 2, gy // 2, gz, gx % 2


def _device(x, y, z, core):
    return ((x // 2) * 2 + core) * 32 + (y * 2 + x % 2) * 4 + z


def _shift(axis0, axis1, k):
    pairs = []
    for d in range(128):
        at = list(_coords(d))
        axis = (axis0, axis1)[at[3]]
        at[axis] = (at[axis] + k) % 4
        pairs.append((d, _device(*at)))
    return pairs


_SIBLING = [(d, d ^ 32) for d in range(128)]
X, Y, Z = 0, 1, 2


def _send(array, pairs):
    return lax.ppermute(array, AXES, pairs)


def _exchange(arrays, axis0, axis1):
    got = {k: _send(arrays[k], _shift(axis0, axis1, k)) for k in (1, 3, 2)}
    return [arrays[0], got[1], got[2], got[3]]


def _position():
    gx, gy, gz = (lax.axis_index(a) for a in AXES)
    core = gx % 2
    x, y = (gx // 2) * 2 + gy % 2, gy // 2
    first, second = jnp.where(core == 0, gz, y), jnp.where(core == 0, y, gz)
    return core, x, y, gz, first, second


def _shape(*dims):
    return jax.ShapeDtypeStruct(dims, F32)


def _params():
    return pltpu.CompilerParams(vmem_limit_bytes=VMEM_LIMIT)


def _block_kernel(k, own, *refs):
    if own:
        p, c, n, got, out, held, sems = refs
    else:
        p, c, n, out, held, sems = refs
    me, _, y, z, _, _ = _position()
    core = me if own else 1 - me
    a = (jnp.where(core == 0, z, y) + k) % 4
    copies = []
    for b in range(4):
        rows = pl.ds(pl.multiple_of(jnp.where(core == 0, a * 8 + b, b * 8 + 4 + a) * 8, 8), 8)
        copies.append([pltpu.make_async_copy(array.at[0, rows], held.at[i, b], sems.at[i, b]) for i, array in enumerate((p, c, n))])
        for copy in copies[b]:
            copy.start()
    for b in range(4):
        for copy in copies[b]:
            copy.wait()
        if own:
            out[0, b] = (held[0, b] + held[1, b]) + got[0, b]
            out[1, b] = held[2, b] + got[1, b]
        else:
            out[0, b] = held[0, b] + held[1, b]
            out[1, b] = held[2, b]


def _block(arrays, k, got=None):
    own = got is not None
    hbm, vmem = pl.BlockSpec(memory_space=pltpu.HBM), pl.BlockSpec(memory_space=pltpu.VMEM)
    return pl.pallas_call(
        functools.partial(_block_kernel, k, own),
        in_specs=[hbm] * 3 + [vmem] * own,
        out_specs=vmem,
        out_shape=_shape(2, 4, 8, 4096),
        scratch_shapes=[pltpu.VMEM((3, 4, 8, 4096), F32), pltpu.SemaphoreType.DMA((3, 4))],
        compiler_params=_params(),
        name="pair_sum" if own else "for_sibling",
    )(*arrays, *([got] if own else []))


def _second_kernel(a, b, c, d, *outs):
    second = _position()[5]
    for k in range(4):
        i = (second + k) % 4
        outs[k][...] = (a[:, i] + b[:, i]) + (c[:, i] + d[:, i])


def _second(parts):
    return pl.pallas_call(
        _second_kernel, out_shape=[_shape(2, 8, 4096)] * 4, compiler_params=_params(), name="first_axis_sum"
    )(*parts)


def _third_kernel(a, b, c, d, *outs):
    x = _position()[1]
    for k in range(4):
        at = pl.ds(pl.multiple_of(((x + k) % 4) * 1024, 1024), 1024)
        outs[k][...] = (a[:, :, at] + b[:, :, at]) + (c[:, :, at] + d[:, :, at])


def _third(parts):
    return pl.pallas_call(
        _third_kernel, out_shape=[_shape(2, 8, 1024)] * 4, compiler_params=_params(), name="second_axis_sum"
    )(*parts)


def _mean_kernel(a, b, c, d, mean, preview):
    both = (a[...] + b[...]) + (c[...] + d[...])
    grid = both[0] / (both[1] + 1.0)
    mean[...] = grid
    four = jnp.concatenate(
        [jnp.sum(grid[0:4], axis=0, keepdims=True), jnp.sum(grid[4:8], axis=0, keepdims=True)], axis=0
    )
    for j in range(2):
        row = lax.broadcasted_iota(jnp.int32, (512, 128), 0)
        column = lax.broadcasted_iota(jnp.int32, (512, 128), 1)
        pool = jnp.where(row // 4 == column, 0.0625, 0.0).astype(F32)
        preview[:, j * 128 : (j + 1) * 128] = jnp.dot(
            four[:, j * 512 : (j + 1) * 512], pool, precision=lax.Precision.HIGHEST, preferred_element_type=F32
        )


def _mean(parts):
    return pl.pallas_call(
        _mean_kernel,
        out_shape=[_shape(8, 1024), _shape(2, 256)],
        compiler_params=_params(),
        name="mean_and_preview",
    )(*parts)


def _pack_kernel(mean, a, b, c, d, out):
    out[:, :1024] = mean[...]
    for k, part in enumerate((a, b, c, d)):
        out[2 * k : 2 * k + 2, 1024:] = part[...]


def _pack(mean, previews):
    return pl.pallas_call(_pack_kernel, out_shape=_shape(8, 1280), compiler_params=_params(), name="pack")(mean, *previews)


def _row_kernel(a, b, c, d, out):
    for k, part in enumerate((a, b, c, d)):
        out[k] = part[...]


def _row(parts):
    return pl.pallas_call(_row_kernel, out_shape=_shape(4, 8, 1280), compiler_params=_params(), name="gathered_row")(*parts)


def _final_kernel(*refs):
    own, other, grid, preview, lines = refs[:4], refs[4:8], refs[8], refs[9], refs[10]
    core, x, y, z, _, _ = _position()
    for mine, parts in ((True, own), (False, other)):
        c = core if mine else 1 - core
        for k2 in range(4):
            for k1 in range(4):
                fy = (y - jnp.where(c == 0, k1, k2)) % 4
                fx = (x - jnp.where(c == 0, k2, k1)) % 4
                rows = pl.multiple_of((c * 4 + fy) * 8, 8)
                columns = pl.multiple_of(fx * 1024, 1024)
                grid[pl.ds(rows, 8), pl.ds(columns, 1024)] = parts[k2][k1, :, :1024]
                for k in range(4):
                    at = pl.ds(pl.multiple_of(fx * 256, 256), 256)
                    lines[(((z - k) % 4) * 2 + c) * 4 + fy, :, at] = parts[k2][k1, 2 * k : 2 * k + 2, 1024:]
    for i in range(8):
        preview[8 * i : 8 * i + 8, :] = jnp.concatenate([lines[4 * i + j] for j in range(4)], axis=0)


def _final(own, other):
    return pl.pallas_call(
        _final_kernel,
        out_shape=[_shape(64, 4096), _shape(64, 1024)],
        scratch_shapes=[pltpu.VMEM((32, 2, 1024), F32)],
        compiler_params=_params(),
        name="assemble",
    )(*own, *other)


def _local(p, c, n):
    arrays = [pltpu.with_memory_space_constraint(array, pltpu.HBM) for array in (p, c, n)]
    order = (1, 3, 2, 0)
    got = {k: _send(_block(arrays, k), _SIBLING) for k in order}
    parts = _exchange({k: _block(arrays, k, got[k]) for k in order}, Z, Y)
    parts = _exchange(_second(parts), Y, Z)
    parts = _exchange(_third(parts), X, X)
    mean, preview = _mean(parts)
    packed = _pack(mean, _exchange([preview] * 4, Z, Z))
    row = _row(_exchange([packed] * 4, Y, X))
    own = _exchange([row] * 4, X, Y)
    other = [_send(part, _SIBLING) for part in own]
    return _final(own, other)


def solution(mesh):
    return jax.shard_map(
        _local,
        mesh=mesh,
        in_specs=(P(AXES, None, None),) * 3,
        out_specs=(P("gz", None), P(None, None)),
        check_vma=False,
    )
```

```python
import functools

import jax
import jax.numpy as jnp
import numpy as np
from jax import lax
from jax.experimental import pallas as pl
from jax.experimental.pallas import tpu as pltpu
from jax.sharding import PartitionSpec as P

AXES = ("gx", "gy", "gz")
F32 = jnp.float32
COST = pl.CostEstimate(flops=1, bytes_accessed=1, transcendentals=0)
VMEM_LIMIT = 20 * 1024 * 1024


def _coords(d):
    gx, gy, gz = d // 32, (d // 4) % 8, d % 4
    return (gx // 2) * 2 + gy % 2, gy // 2, gz, gx % 2


def _device(x, y, z, core):
    return ((x // 2) * 2 + core) * 32 + (y * 2 + x % 2) * 4 + z


X, Y, Z = 0, 1, 2


X, Y, Z = 0, 1, 2


def _shift(k, axis0, axis1):
    pairs = []
    for d in range(128):
        at = list(_coords(d))
        axis = (axis0, axis1)[at[3]]
        at[axis] = (at[axis] + k) % 4
        pairs.append((d, _device(*at)))
    return pairs


_SIBLING = [(d, d ^ 32) for d in range(128)]


def _send(array, pairs):
    return lax.ppermute(array, AXES, pairs)


def _exchange(arrays, *axes):
    got = {k: _send(arrays[k], _shift(k, *axes)) for k in (1, 3, 2)}
    return [arrays[0], got[1], got[2], got[3]]


def _position():
    gx, gy, gz = (lax.axis_index(a) for a in AXES)
    core = gx % 2
    x, y = (gx // 2) * 2 + gy % 2, gy // 2
    first, second = jnp.where(core == 0, gz, y), jnp.where(core == 0, y, gz)
    return core, x, y, gz, first, second


def _shape(*dims):
    return jax.ShapeDtypeStruct(dims, F32)


def _params():
    return pltpu.CompilerParams(vmem_limit_bytes=VMEM_LIMIT)


def _blocks_kernel(wanted, *refs):
    p, c, n = refs[:3]
    outs, held, sems = refs[-2 - len(wanted) : -2], refs[-2], refs[-1]
    me, _, y, z, _, _ = _position()
    copies = []
    for j, (k, own) in enumerate(wanted):
        core = me if own else 1 - me
        a = (jnp.where(core == 0, z, y) + k) % 4
        for b in range(4):
            rows = pl.ds(pl.multiple_of(jnp.where(core == 0, a * 8 + b, b * 8 + 4 + a) * 8, 8), 8)
            for i, array in enumerate((p, c, n)):
                copy = pltpu.make_async_copy(array.at[0, rows], held.at[i, j, b], sems.at[i, j, b])
                copy.start()
                copies.append((i, j, b, copy))
    for i, j, b, copy in copies:
        copy.wait()
        if i == 2:
            outs[j][0, b] = held[0, j, b] + held[1, j, b]
            outs[j][1, b] = held[2, j, b]


def _blocks(arrays, wanted, after=()):
    return pl.pallas_call(
        functools.partial(_blocks_kernel, wanted),
        in_specs=[pl.BlockSpec(memory_space=pltpu.HBM)] * 3 + [pl.BlockSpec(memory_space=pl.ANY)] * len(after),
        out_shape=[_shape(2, 4, 8, 4096)] * len(wanted),
        scratch_shapes=[pltpu.VMEM((3, len(wanted), 4, 8, 4096), F32), pltpu.SemaphoreType.DMA((3, len(wanted), 4))],
        compiler_params=_params(),
        cost_estimate=COST,
        name="local_blocks",
    )(*arrays, *after)


LOW, HIGH = slice(0, 2), slice(2, 4)


def _sums_kernel(terms, *refs):
    outs = refs[len(refs) - len(terms) :]
    for out, pairs in zip(outs, terms):
        total = refs[pairs[0][0]][:, pairs[0][1]]
        for i, part in pairs[1:]:
            total = total + refs[i][:, part]
        out[...] = total


def _sums(inputs, terms, name, after=()):
    return pl.pallas_call(
        functools.partial(_sums_kernel, terms),
        in_specs=[pl.BlockSpec()] * len(inputs) + [pl.BlockSpec(memory_space=pl.ANY)] * len(after),
        out_shape=[_shape(2, 2, 8, 4096)] * len(terms),
        compiler_params=_params(),
        cost_estimate=COST,
        name=name,
    )(*inputs, *after)


def _second_kernel(low, high, got, low1, high3, *outs):
    second = _position()[5]
    for k in range(4):
        i = (second + k) % 4

        @pl.when(i < 2)
        def _():
            outs[k][...] = (low[:, i] + got[:, i]) + low1[:, i]

        @pl.when(i >= 2)
        def _():
            outs[k][...] = (high[:, i - 2] + got[:, i]) + high3[:, i - 2]


def _second(*parts):
    return pl.pallas_call(
        _second_kernel, out_shape=[_shape(2, 8, 4096)] * 4, compiler_params=_params(), cost_estimate=COST, name="first_axis_sum"
    )(*parts)


def _third_kernel(a, b, c, d, *outs):
    x = _position()[1]
    for k in range(4):
        at = pl.ds(pl.multiple_of(((x + k) % 4) * 1024, 1024), 1024)
        outs[k][...] = (a[:, :, at] + b[:, :, at]) + (c[:, :, at] + d[:, :, at])


def _third(parts):
    return pl.pallas_call(
        _third_kernel, out_shape=[_shape(2, 8, 1024)] * 4, compiler_params=_params(), cost_estimate=COST, name="second_axis_sum"
    )(*parts)


def _mean_kernel(a, b, c, d, mean, preview):
    both = (a[...] + b[...]) + (c[...] + d[...])
    grid = both[0] / (both[1] + 1.0)
    mean[...] = grid
    four = jnp.concatenate(
        [jnp.sum(grid[0:4], axis=0, keepdims=True), jnp.sum(grid[4:8], axis=0, keepdims=True)], axis=0
    )
    for j in range(2):
        row = lax.broadcasted_iota(jnp.int32, (512, 128), 0)
        column = lax.broadcasted_iota(jnp.int32, (512, 128), 1)
        pool = jnp.where(row // 4 == column, 0.0625, 0.0).astype(F32)
        preview[:, j * 128 : (j + 1) * 128] = jnp.dot(
            four[:, j * 512 : (j + 1) * 512], pool, precision=lax.Precision.HIGHEST, preferred_element_type=F32
        )


def _mean(parts):
    return pl.pallas_call(
        _mean_kernel,
        out_shape=[_shape(8, 1024), _shape(2, 256)],
        compiler_params=_params(),
        cost_estimate=COST,
        name="mean_and_preview",
    )(*parts)


def _pack_kernel(mean, a, b, c, d, out):
    out[:, :1024] = mean[...]
    for k, part in enumerate((a, b, c, d)):
        out[2 * k : 2 * k + 2, 1024:] = part[...]


def _pack(mean, previews):
    return pl.pallas_call(_pack_kernel, out_shape=_shape(8, 1280), compiler_params=_params(), cost_estimate=COST, name="pack")(mean, *previews)


def _row_kernel(a, b, c, d, out):
    for k, part in enumerate((a, b, c, d)):
        out[k] = part[...]


def _row(parts):
    return pl.pallas_call(_row_kernel, out_shape=_shape(4, 8, 1280), compiler_params=_params(), cost_estimate=COST, name="gathered_row")(*parts)


def _final_kernel(*refs):
    own, other, grid, preview, lines = refs[:4], refs[4:8], refs[8], refs[9], refs[10]
    core, x, y, z, _, _ = _position()
    for mine, parts in ((True, own), (False, other)):
        c = core if mine else 1 - core
        for k2 in range(4):
            for k1 in range(4):
                fy = (y - jnp.where(c == 0, k1, k2)) % 4
                fx = (x - jnp.where(c == 0, k2, k1)) % 4
                rows = pl.multiple_of((c * 4 + fy) * 8, 8)
                columns = pl.multiple_of(fx * 1024, 1024)
                grid[pl.ds(rows, 8), pl.ds(columns, 1024)] = parts[k2][k1, :, :1024]
                for k in range(4):
                    at = pl.ds(pl.multiple_of(fx * 256, 256), 256)
                    lines[(((z - k) % 4) * 2 + c) * 4 + fy, :, at] = parts[k2][k1, 2 * k : 2 * k + 2, 1024:]
    for i in range(8):
        preview[8 * i : 8 * i + 8, :] = jnp.concatenate([lines[4 * i + j] for j in range(4)], axis=0)


def _final(own, other):
    return pl.pallas_call(
        _final_kernel,
        out_shape=[_shape(64, 4096), _shape(64, 1024)],
        scratch_shapes=[pltpu.VMEM((32, 2, 1024), F32)],
        compiler_params=_params(),
        cost_estimate=COST,
        name="assemble",
    )(*own, *other)


def _first_axis(arrays):
    up, down = _shift(1, Z, Y), _shift(3, Z, Y)
    whole = slice(None)
    sent2, own2 = _blocks(arrays, ((2, False), (2, True)))
    got2 = _send(sent2, _SIBLING)
    sent1, sent3 = _blocks(arrays, ((1, False), (3, False)), (own2,))
    got1, got3 = _send(sent1, _SIBLING), _send(sent3, _SIBLING)
    low2, high2 = _sums((own2, got2), [[(0, LOW), (1, LOW)], [(0, HIGH), (1, HIGH)]], "opposite_pair", (sent1,))
    low, high = _send(low2, up), _send(high2, down)
    own1, own3, sent0, own0 = _blocks(arrays, ((1, True), (3, True), (0, False), (0, True)), (low2,))
    low1, high1, low3, high3 = _sums(
        (own1, got1, own3, got3),
        [[(0, LOW), (1, LOW)], [(0, HIGH), (1, HIGH)], [(2, LOW), (3, LOW)], [(2, HIGH), (3, HIGH)]],
        "neighbour_pairs",
    )
    got0 = _send(sent0, _SIBLING)
    high1, low3 = _send(high1, up), _send(low3, down)
    low1, high3 = _sums((low1, low, high3, high), [[(0, whole), (1, whole)], [(2, whole), (3, whole)]], "passed_on")
    low, high = _sums(
        (own0, low3, high1),
        [[(0, LOW), (1, whole)], [(0, HIGH), (2, whole)]],
        "early_sum",
    )
    return _second(low, high, got0, _send(low1, up), _send(high3, down))


def _local(p, c, n):
    arrays = [pltpu.with_memory_space_constraint(array, pltpu.HBM) for array in (p, c, n)]
    parts = _exchange(_first_axis(arrays), Y, Z)
    parts = _exchange(_third(parts), X, X)
    mean, preview = _mean(parts)
    packed = _pack(mean, _exchange([preview] * 4, Z, Z))
    row = _row(_exchange([packed] * 4, Y, X))
    own = _exchange([row] * 4, X, Y)
    other = [_send(part, _SIBLING) for part in own]
    return _final(own, other)


def solution(mesh):
    return jax.shard_map(
        _local,
        mesh=mesh,
        in_specs=(P(AXES, None, None),) * 3,
        out_specs=(P("gz", None), P(None, None)),
        check_vma=False,
    )
```

```python
import functools

import jax
import jax.numpy as jnp
import numpy as np
from jax import lax
from jax.experimental import pallas as pl
from jax.experimental.pallas import tpu as pltpu
from jax.sharding import PartitionSpec as P

AXES = ("gx", "gy", "gz")
F32 = jnp.float32
COST = pl.CostEstimate(flops=1, bytes_accessed=1, transcendentals=0)
VMEM_LIMIT = 20 * 1024 * 1024


def _coords(d):
    gx, gy, gz = d // 32, (d // 4) % 8, d % 4
    return (gx // 2) * 2 + gy % 2, gy // 2, gz, gx % 2


def _device(x, y, z, core):
    return ((x // 2) * 2 + core) * 32 + (y * 2 + x % 2) * 4 + z


X, Y, Z = 0, 1, 2


X, Y, Z = 0, 1, 2


def _shift(k, axis0, axis1):
    pairs = []
    for d in range(128):
        at = list(_coords(d))
        axis = (axis0, axis1)[at[3]]
        at[axis] = (at[axis] + k) % 4
        pairs.append((d, _device(*at)))
    return pairs


_SIBLING = [(d, d ^ 32) for d in range(128)]


def _send(array, pairs):
    return lax.ppermute(array, AXES, pairs)


def _exchange(arrays, *axes):
    got = {k: _send(arrays[k], _shift(k, *axes)) for k in (1, 3, 2)}
    return [arrays[0], got[1], got[2], got[3]]


def _position():
    gx, gy, gz = (lax.axis_index(a) for a in AXES)
    core = gx % 2
    x, y = (gx // 2) * 2 + gy % 2, gy // 2
    first, second = jnp.where(core == 0, gz, y), jnp.where(core == 0, y, gz)
    return core, x, y, gz, first, second


def _shape(*dims):
    return jax.ShapeDtypeStruct(dims, F32)


def _params():
    return pltpu.CompilerParams(vmem_limit_bytes=VMEM_LIMIT)


def _blocks_kernel(wanted, *refs):
    p, c, n = refs[:3]
    outs, held, sems = refs[-2 - len(wanted) : -2], refs[-2], refs[-1]
    me, _, y, z, _, _ = _position()
    copies = []
    for j, (k, own) in enumerate(wanted):
        core = me if own else 1 - me
        a = (jnp.where(core == 0, z, y) + k) % 4
        for b in range(4):
            rows = pl.ds(pl.multiple_of(jnp.where(core == 0, a * 8 + b, b * 8 + 4 + a) * 8, 8), 8)
            for i, array in enumerate((p, c, n)):
                copy = pltpu.make_async_copy(array.at[0, rows], held.at[i, j, b], sems.at[i, j, b])
                copy.start()
                copies.append((i, j, b, copy))
    for i, j, b, copy in copies:
        copy.wait()
        if i == 2:
            outs[j][0, b] = held[0, j, b] + held[1, j, b]
            outs[j][1, b] = held[2, j, b]


def _blocks(arrays, wanted, after=()):
    return pl.pallas_call(
        functools.partial(_blocks_kernel, wanted),
        in_specs=[pl.BlockSpec(memory_space=pltpu.HBM)] * 3 + [pl.BlockSpec(memory_space=pl.ANY)] * len(after),
        out_shape=[_shape(2, 4, 8, 4096)] * len(wanted),
        scratch_shapes=[pltpu.VMEM((3, len(wanted), 4, 8, 4096), F32), pltpu.SemaphoreType.DMA((3, len(wanted), 4))],
        compiler_params=_params(),
        cost_estimate=COST,
        name="local_blocks",
    )(*arrays, *after)


LOW, HIGH = slice(0, 2), slice(2, 4)


def _sums_kernel(terms, *refs):
    outs = refs[len(refs) - len(terms) :]
    for out, pairs in zip(outs, terms):
        total = refs[pairs[0][0]][:, pairs[0][1]]
        for i, part in pairs[1:]:
            total = total + refs[i][:, part]
        out[...] = total


def _sums(inputs, terms, name, after=()):
    return pl.pallas_call(
        functools.partial(_sums_kernel, terms),
        in_specs=[pl.BlockSpec()] * len(inputs) + [pl.BlockSpec(memory_space=pl.ANY)] * len(after),
        out_shape=[_shape(2, 2, 8, 4096)] * len(terms),
        compiler_params=_params(),
        cost_estimate=COST,
        name=name,
    )(*inputs, *after)


def _second_kernel(low, high, got, low1, high3, *outs):
    core, x, y, _, _, _ = _position()
    for k in range(4):
        i = (y + k) % 4

        @pl.when((core == 0) & (i < 2))
        def _():
            total = (low[:, i] + got[:, i]) + low1[:, i]
            for j in range(4):
                outs[k][:, j] = total[:, :, j * 1024 : (j + 1) * 1024]

        @pl.when((core == 0) & (i >= 2))
        def _():
            total = (high[:, i - 2] + got[:, i]) + high3[:, i - 2]
            for j in range(4):
                outs[k][:, j] = total[:, :, j * 1024 : (j + 1) * 1024]

        @pl.when(core == 1)
        def _():
            at = pl.ds(pl.multiple_of(((x + k) % 4) * 1024, 1024), 1024)
            for j in range(2):
                outs[k][:, j] = (low[:, j, :, at] + got[:, j, :, at]) + low1[:, j, :, at]
                outs[k][:, j + 2] = (high[:, j, :, at] + got[:, j + 2, :, at]) + high3[:, j, :, at]


def _second(*parts):
    return pl.pallas_call(
        _second_kernel, out_shape=[_shape(2, 4, 8, 1024)] * 4, compiler_params=_params(), cost_estimate=COST, name="first_axis_sum"
    )(*parts)


def _third_kernel(a, b, c, d, out):
    out[...] = (a[...] + b[...]) + (c[...] + d[...])


def _third(parts):
    return pl.pallas_call(
        _third_kernel, out_shape=_shape(2, 4, 8, 1024), compiler_params=_params(), cost_estimate=COST, name="second_axis_sum"
    )(*parts)


def _mean_kernel(a, b, c, d, out, means):
    core, _, _, z, _, _ = _position()
    lines = []
    for j in range(4):
        total = (a[0, j] + b[0, j]) + (c[0, j] + d[0, j])
        count = (a[1, j] + b[1, j]) + (c[1, j] + d[1, j])
        means[j] = total / (count + 1.0)
        lines += [jnp.sum(means[j, 0:4], axis=0, keepdims=True), jnp.sum(means[j, 4:8], axis=0, keepdims=True)]
    four = jnp.concatenate(lines, axis=0)
    row = lax.broadcasted_iota(jnp.int32, (512, 128), 0)
    column = lax.broadcasted_iota(jnp.int32, (512, 128), 1)
    pool = jnp.where(row // 4 == column, 0.0625, 0.0).astype(F32)
    for j in range(4):
        out[j, :, :1024] = means[jnp.where(core == 0, j, (z + j) % 4)]
        out[j, :, 1024:] = jnp.zeros((8, 256), F32)
    for j in range(2):
        out[0, :, 1024 + j * 128 : 1024 + (j + 1) * 128] = jnp.dot(
            four[:, j * 512 : (j + 1) * 512], pool, precision=lax.Precision.HIGHEST, preferred_element_type=F32
        )


def _mean(parts):
    return pl.pallas_call(
        _mean_kernel,
        out_shape=_shape(4, 8, 1280),
        scratch_shapes=[pltpu.VMEM((4, 8, 1024), F32)],
        compiler_params=_params(),
        cost_estimate=COST,
        name="mean_and_preview",
    )(*parts)


def _row_kernel(a, b, c, d, out):
    for k, part in enumerate((a, b, c, d)):
        out[k] = part[0]


def _row(parts):
    return pl.pallas_call(
        _row_kernel, out_shape=_shape(4, 8, 1280), compiler_params=_params(), cost_estimate=COST, name="gathered_row"
    )(*parts)


def _final_kernel(*refs):
    own_rows, other_rows, own, other = (refs[4 * i : 4 * i + 4] for i in range(4))
    grid, preview, lines = refs[16:]
    me, x, y, z, _, _ = _position()

    def place(rows0, last0, last1):
        for k in range(4):
            fy = (y - k) % 4
            for j in range(4):
                grid[pl.ds(pl.multiple_of(fy * 8, 8), 8), j * 1024 : (j + 1) * 1024] = rows0[k][j, :, :1024]
            fz = (z - k) % 4
            for i in range(4):
                for j in range(4):
                    lines[fz * 8 + (y - i) % 4, :, j * 256 : (j + 1) * 256] = last0[k][i, 2 * j : 2 * j + 2, 1024:]
            for i in range(4):
                fx = (x - i) % 4
                columns = pl.ds(pl.multiple_of(fx * 1024, 1024), 1024)
                grid[pl.ds(pl.multiple_of(32 + fy * 8, 8), 8), columns] = last1[k][i, :, :1024]
                at = pl.ds(pl.multiple_of(fx * 256, 256), 256)
                for j in range(4):
                    lines[j * 8 + 4 + fy, :, at] = last1[k][i, 2 * j : 2 * j + 2, 1024:]

    @pl.when(me == 0)
    def _():
        place(own_rows, own, other)

    @pl.when(me == 1)
    def _():
        place(other_rows, other, own)

    for i in range(8):
        preview[8 * i : 8 * i + 8, :] = jnp.concatenate([lines[4 * i + j] for j in range(4)], axis=0)


def _final(own_rows, other_rows, own, other):
    return pl.pallas_call(
        _final_kernel,
        out_shape=[_shape(64, 4096), _shape(64, 1024)],
        scratch_shapes=[pltpu.VMEM((32, 2, 1024), F32)],
        compiler_params=_params(),
        cost_estimate=COST,
        name="assemble",
    )(*own_rows, *other_rows, *own, *other)


def _first_axis(arrays):
    up, down = _shift(1, Z, Y), _shift(3, Z, Y)
    whole = slice(None)
    sent2, own2 = _blocks(arrays, ((2, False), (2, True)))
    got2 = _send(sent2, _SIBLING)
    sent1, sent3 = _blocks(arrays, ((1, False), (3, False)), (own2,))
    got1, got3 = _send(sent1, _SIBLING), _send(sent3, _SIBLING)
    low2, high2 = _sums((own2, got2), [[(0, LOW), (1, LOW)], [(0, HIGH), (1, HIGH)]], "opposite_pair", (sent1,))
    low, high = _send(low2, up), _send(high2, down)
    own1, own3, sent0, own0 = _blocks(arrays, ((1, True), (3, True), (0, False), (0, True)), (low2,))
    low1, high1, low3, high3 = _sums(
        (own1, got1, own3, got3),
        [[(0, LOW), (1, LOW)], [(0, HIGH), (1, HIGH)], [(2, LOW), (3, LOW)], [(2, HIGH), (3, HIGH)]],
        "neighbour_pairs",
    )
    got0 = _send(sent0, _SIBLING)
    high1, low3 = _send(high1, up), _send(low3, down)
    low1, high3 = _sums((low1, low, high3, high), [[(0, whole), (1, whole)], [(2, whole), (3, whole)]], "passed_on")
    low, high = _sums(
        (own0, low3, high1),
        [[(0, LOW), (1, whole)], [(0, HIGH), (2, whole)]],
        "early_sum",
    )
    return _second(low, high, got0, _send(low1, up), _send(high3, down))


def _local(p, c, n):
    arrays = [pltpu.with_memory_space_constraint(array, pltpu.HBM) for array in (p, c, n)]
    both = _third(_exchange(_first_axis(arrays), Y, X))
    packed = _mean(_exchange([both] * 4, X, Z))
    rows = _exchange([packed] * 4, Y, X)
    last = _exchange([_row(rows)] * 4, Z, Y)
    return _final(rows, [_send(part, _SIBLING) for part in rows], last, [_send(part, _SIBLING) for part in last])


def solution(mesh):
    return jax.shard_map(
        _local,
        mesh=mesh,
        in_specs=(P(AXES, None, None),) * 3,
        out_specs=(P("gz", None), P(None, None)),
        check_vma=False,
    )
```

```python
import functools

import jax
import jax.numpy as jnp
import numpy as np
from jax import lax
from jax.experimental import pallas as pl
from jax.experimental.pallas import tpu as pltpu
from jax.sharding import PartitionSpec as P

AXES = ("gx", "gy", "gz")
F32 = jnp.float32
COST = pl.CostEstimate(flops=1, bytes_accessed=1, transcendentals=0)
VMEM_LIMIT = 20 * 1024 * 1024


def _coords(d):
    gx, gy, gz = d // 32, (d // 4) % 8, d % 4
    return (gx // 2) * 2 + gy % 2, gy // 2, gz, gx % 2


def _device(x, y, z, core):
    return ((x // 2) * 2 + core) * 32 + (y * 2 + x % 2) * 4 + z


X, Y, Z = 0, 1, 2


X, Y, Z = 0, 1, 2


def _shift(k, axis0, axis1):
    pairs = []
    for d in range(128):
        at = list(_coords(d))
        axis = (axis0, axis1)[at[3]]
        at[axis] = (at[axis] + k) % 4
        pairs.append((d, _device(*at)))
    return pairs


_SIBLING = [(d, d ^ 32) for d in range(128)]


def _send(array, pairs):
    return lax.ppermute(array, AXES, pairs)


def _partner(k, axis0, axis1):
    pairs = []
    for d in range(128):
        at = list(_coords(d))
        at[(axis0, axis1)[at[3]]] ^= k
        pairs.append((d, _device(*at)))
    return pairs


def _exchange(arrays, axis0, axis1, pairs=_partner):
    got = {k: _send(arrays[k], pairs(k, axis0, axis1)) for k in (1, 3, 2)}
    return [arrays[0], got[1], got[2], got[3]]


def _position():
    gx, gy, gz = (lax.axis_index(a) for a in AXES)
    core = gx % 2
    x, y = (gx // 2) * 2 + gy % 2, gy // 2
    first, second = jnp.where(core == 0, gz, y), jnp.where(core == 0, y, gz)
    return core, x, y, gz, first, second


def _shape(*dims):
    return jax.ShapeDtypeStruct(dims, F32)


def _params():
    return pltpu.CompilerParams(vmem_limit_bytes=VMEM_LIMIT)


def _blocks_kernel(wanted, *refs):
    p, c, n = refs[:3]
    outs, held, sems = refs[-2 - len(wanted) : -2], refs[-2], refs[-1]
    me, _, y, z, _, _ = _position()
    copies = []
    for j, (k, own) in enumerate(wanted):
        core = me if own else 1 - me
        a = (jnp.where(core == 0, z, y) + k) % 4
        for b in range(4):
            rows = pl.ds(pl.multiple_of(jnp.where(core == 0, a * 8 + b, b * 8 + 4 + a) * 8, 8), 8)
            for i, array in enumerate((p, c, n)):
                copy = pltpu.make_async_copy(array.at[0, rows], held.at[i, j, b], sems.at[i, j, b])
                copy.start()
                copies.append((i, j, b, copy))
    for i, j, b, copy in copies:
        copy.wait()
        if i == 2:
            outs[j][0, b] = held[0, j, b] + held[1, j, b]
            outs[j][1, b] = held[2, j, b]


def _blocks(arrays, wanted, after=()):
    return pl.pallas_call(
        functools.partial(_blocks_kernel, wanted),
        in_specs=[pl.BlockSpec(memory_space=pltpu.HBM)] * 3 + [pl.BlockSpec(memory_space=pl.ANY)] * len(after),
        out_shape=[_shape(2, 4, 8, 4096)] * len(wanted),
        scratch_shapes=[pltpu.VMEM((3, len(wanted), 4, 8, 4096), F32), pltpu.SemaphoreType.DMA((3, len(wanted), 4))],
        compiler_params=_params(),
        cost_estimate=COST,
        name="local_blocks",
    )(*arrays, *after)


LOW, HIGH = slice(0, 2), slice(2, 4)


def _sums_kernel(terms, *refs):
    outs = refs[len(refs) - len(terms) :]
    for out, pairs in zip(outs, terms):
        total = refs[pairs[0][0]][:, pairs[0][1]]
        for i, part in pairs[1:]:
            total = total + refs[i][:, part]
        out[...] = total


def _sums(inputs, terms, name, after=()):
    return pl.pallas_call(
        functools.partial(_sums_kernel, terms),
        in_specs=[pl.BlockSpec()] * len(inputs) + [pl.BlockSpec(memory_space=pl.ANY)] * len(after),
        out_shape=[_shape(2, 2, 8, 4096)] * len(terms),
        compiler_params=_params(),
        cost_estimate=COST,
        name=name,
    )(*inputs, *after)


def _second_kernel(low, high, got, low1, high3, *outs):
    core, x, y, _, _, _ = _position()
    for k in range(4):
        i = (y + k) % 4

        @pl.when((core == 0) & (i < 2))
        def _():
            total = (low[:, i] + got[:, i]) + low1[:, i]
            for j in range(4):
                outs[k][:, j] = total[:, :, j * 1024 : (j + 1) * 1024]

        @pl.when((core == 0) & (i >= 2))
        def _():
            total = (high[:, i - 2] + got[:, i]) + high3[:, i - 2]
            for j in range(4):
                outs[k][:, j] = total[:, :, j * 1024 : (j + 1) * 1024]

        @pl.when(core == 1)
        def _():
            at = pl.ds(pl.multiple_of(((x + k) % 4) * 1024, 1024), 1024)
            for j in range(2):
                outs[k][:, j] = (low[:, j, :, at] + got[:, j, :, at]) + low1[:, j, :, at]
                outs[k][:, j + 2] = (high[:, j, :, at] + got[:, j + 2, :, at]) + high3[:, j, :, at]


def _second(*parts):
    return pl.pallas_call(
        _second_kernel, out_shape=[_shape(2, 4, 8, 1024)] * 4, compiler_params=_params(), cost_estimate=COST, name="first_axis_sum"
    )(*parts)


def _third_kernel(a, b, c, d, out):
    out[...] = (a[...] + b[...]) + (c[...] + d[...])


def _third(parts):
    return pl.pallas_call(
        _third_kernel, out_shape=_shape(2, 4, 8, 1024), compiler_params=_params(), cost_estimate=COST, name="second_axis_sum"
    )(*parts)


def _mean_kernel(a, b, c, d, out, means):
    core, _, _, z, _, _ = _position()
    lines = []
    for j in range(4):
        total = (a[0, j] + b[0, j]) + (c[0, j] + d[0, j])
        count = (a[1, j] + b[1, j]) + (c[1, j] + d[1, j])
        means[j] = total / (count + 1.0)
        lines += [jnp.sum(means[j, 0:4], axis=0, keepdims=True), jnp.sum(means[j, 4:8], axis=0, keepdims=True)]
    four = jnp.concatenate(lines, axis=0)
    row = lax.broadcasted_iota(jnp.int32, (512, 128), 0)
    column = lax.broadcasted_iota(jnp.int32, (512, 128), 1)
    pool = jnp.where(row // 4 == column, 0.0625, 0.0).astype(F32)
    for j in range(4):
        out[:, j * 1024 : (j + 1) * 1024] = means[jnp.where(core == 0, j, z ^ j)]
    for j in range(2):
        out[:, 4096 + j * 128 : 4096 + (j + 1) * 128] = jnp.dot(
            four[:, j * 512 : (j + 1) * 512], pool, precision=lax.Precision.HIGHEST, preferred_element_type=F32
        )


def _mean(parts):
    return pl.pallas_call(
        _mean_kernel,
        out_shape=_shape(8, 4352),
        scratch_shapes=[pltpu.VMEM((4, 8, 1024), F32)],
        compiler_params=_params(),
        cost_estimate=COST,
        name="mean_and_preview",
    )(*parts)


def _row_kernel(a, b, c, d, out):
    for k, part in enumerate((a, b, c, d)):
        out[k, :, :1024] = part[:, :1024]
        out[k, :, 1024:] = part[:, 4096:]


def _row(parts):
    return pl.pallas_call(
        _row_kernel, out_shape=_shape(4, 8, 1280), compiler_params=_params(), cost_estimate=COST, name="gathered_row"
    )(*parts)


def _final_kernel(*refs):
    own_rows, other_rows, own, other = (refs[4 * i : 4 * i + 4] for i in range(4))
    grid, preview, lines = refs[16:]
    me, x, y, z, _, _ = _position()

    def place(rows0, last0, last1):
        for k in range(4):
            fy, fz = y ^ k, z ^ k
            grid[pl.ds(pl.multiple_of(fy * 8, 8), 8), :] = rows0[k][:, :4096]
            for i in range(4):
                for j in range(4):
                    lines[fz * 8 + (y ^ i), :, j * 256 : (j + 1) * 256] = last0[k][i, 2 * j : 2 * j + 2, 1024:]
            for i in range(4):
                fx = x ^ i
                columns = pl.ds(pl.multiple_of(fx * 1024, 1024), 1024)
                grid[pl.ds(pl.multiple_of(32 + fy * 8, 8), 8), columns] = last1[k][i, :, :1024]
                at = pl.ds(pl.multiple_of(fx * 256, 256), 256)
                for j in range(4):
                    lines[j * 8 + 4 + fy, :, at] = last1[k][i, 2 * j : 2 * j + 2, 1024:]

    @pl.when(me == 0)
    def _():
        place(own_rows, own, other)

    @pl.when(me == 1)
    def _():
        place(other_rows, other, own)

    for i in range(8):
        preview[8 * i : 8 * i + 8, :] = jnp.concatenate([lines[4 * i + j] for j in range(4)], axis=0)


def _final(own_rows, other_rows, own, other):
    return pl.pallas_call(
        _final_kernel,
        out_shape=[_shape(64, 4096), _shape(64, 1024)],
        scratch_shapes=[pltpu.VMEM((32, 2, 1024), F32)],
        compiler_params=_params(),
        cost_estimate=COST,
        name="assemble",
    )(*own_rows, *other_rows, *own, *other)


def _first_axis(arrays):
    up, down = _shift(1, Z, Y), _shift(3, Z, Y)
    whole = slice(None)
    sent2, own2 = _blocks(arrays, ((2, False), (2, True)))
    got2 = _send(sent2, _SIBLING)
    sent1, sent3 = _blocks(arrays, ((1, False), (3, False)), (own2,))
    got1, got3 = _send(sent1, _SIBLING), _send(sent3, _SIBLING)
    low2, high2 = _sums((own2, got2), [[(0, LOW), (1, LOW)], [(0, HIGH), (1, HIGH)]], "opposite_pair", (sent1,))
    low, high = _send(low2, up), _send(high2, down)
    own1, own3, sent0, own0 = _blocks(arrays, ((1, True), (3, True), (0, False), (0, True)), (low2,))
    low1, high1, low3, high3 = _sums(
        (own1, got1, own3, got3),
        [[(0, LOW), (1, LOW)], [(0, HIGH), (1, HIGH)], [(2, LOW), (3, LOW)], [(2, HIGH), (3, HIGH)]],
        "neighbour_pairs",
    )
    got0 = _send(sent0, _SIBLING)
    high1, low3 = _send(high1, up), _send(low3, down)
    low1, high3 = _sums((low1, low, high3, high), [[(0, whole), (1, whole)], [(2, whole), (3, whole)]], "passed_on")
    low, high = _sums(
        (own0, low3, high1),
        [[(0, LOW), (1, whole)], [(0, HIGH), (2, whole)]],
        "early_sum",
    )
    return _second(low, high, got0, _send(low1, up), _send(high3, down))


def _local(p, c, n):
    arrays = [pltpu.with_memory_space_constraint(array, pltpu.HBM) for array in (p, c, n)]
    both = _third(_exchange(_first_axis(arrays), Y, X, _shift))
    packed = _mean(_exchange([both] * 4, X, Z))
    rows = _exchange([packed] * 4, Y, X)
    last = _exchange([_row(rows)] * 4, Z, Y)
    return _final(rows, [_send(part, _SIBLING) for part in rows], last, [_send(part, _SIBLING) for part in last])


def solution(mesh):
    return jax.shard_map(
        _local,
        mesh=mesh,
        in_specs=(P(AXES, None, None),) * 3,
        out_specs=(P("gz", None), P(None, None)),
        check_vma=False,
    )
```

```python
import functools

import jax
import jax.numpy as jnp
import numpy as np
from jax import lax
from jax.experimental import pallas as pl
from jax.experimental.pallas import tpu as pltpu
from jax.sharding import PartitionSpec as P

AXES = ("gx", "gy", "gz")
F32 = jnp.float32
COST = pl.CostEstimate(flops=1, bytes_accessed=1, transcendentals=0)
VMEM_LIMIT = 20 * 1024 * 1024


def _coords(d):
    gx, gy, gz = d // 32, (d // 4) % 8, d % 4
    return (gx // 2) * 2 + gy % 2, gy // 2, gz, gx % 2


def _device(x, y, z, core):
    return ((x // 2) * 2 + core) * 32 + (y * 2 + x % 2) * 4 + z


X, Y, Z = 0, 1, 2


X, Y, Z = 0, 1, 2


def _shift(k, axis0, axis1):
    pairs = []
    for d in range(128):
        at = list(_coords(d))
        axis = (axis0, axis1)[at[3]]
        at[axis] = (at[axis] + k) % 4
        pairs.append((d, _device(*at)))
    return pairs


_SIBLING = [(d, d ^ 32) for d in range(128)]


def _send(array, pairs):
    return lax.ppermute(array, AXES, pairs)


def _partner(k, axis0, axis1):
    pairs = []
    for d in range(128):
        at = list(_coords(d))
        at[(axis0, axis1)[at[3]]] ^= k
        pairs.append((d, _device(*at)))
    return pairs


def _exchange(arrays, axis0, axis1, pairs=_partner):
    got = {k: _send(arrays[k], pairs(k, axis0, axis1)) for k in (1, 3, 2)}
    return [arrays[0], got[1], got[2], got[3]]


def _position():
    gx, gy, gz = (lax.axis_index(a) for a in AXES)
    core = gx % 2
    x, y = (gx // 2) * 2 + gy % 2, gy // 2
    first, second = jnp.where(core == 0, gz, y), jnp.where(core == 0, y, gz)
    return core, x, y, gz, first, second


def _shape(*dims):
    return jax.ShapeDtypeStruct(dims, F32)


def _params():
    return pltpu.CompilerParams(vmem_limit_bytes=VMEM_LIMIT)


def _blocks_kernel(wanted, *refs):
    p, c, n = refs[:3]
    outs, held, sems = refs[-2 - len(wanted) : -2], refs[-2], refs[-1]
    me, _, y, z, _, _ = _position()
    copies = []
    for j, (k, own) in enumerate(wanted):
        core = me if own else 1 - me
        a = jnp.where(core == 0, z, y) ^ k
        for b in range(4):
            rows = pl.ds(pl.multiple_of(jnp.where(core == 0, a * 8 + b, b * 8 + 4 + a) * 8, 8), 8)
            for i, array in enumerate((p, c, n)):
                copy = pltpu.make_async_copy(array.at[0, rows], held.at[i, j, b], sems.at[i, j, b])
                copy.start()
                copies.append((i, j, b, copy))
    for i, j, b, copy in copies:
        copy.wait()
        if i == 2:
            outs[j][0, b] = held[0, j, b] + held[1, j, b]
            outs[j][1, b] = held[2, j, b]


def _blocks(arrays, wanted, after=()):
    return pl.pallas_call(
        functools.partial(_blocks_kernel, wanted),
        in_specs=[pl.BlockSpec(memory_space=pltpu.HBM)] * 3 + [pl.BlockSpec(memory_space=pl.ANY)] * len(after),
        out_shape=[_shape(2, 4, 8, 4096)] * len(wanted),
        scratch_shapes=[pltpu.VMEM((3, len(wanted), 4, 8, 4096), F32), pltpu.SemaphoreType.DMA((3, len(wanted), 4))],
        compiler_params=_params(),
        cost_estimate=COST,
        name="local_blocks",
    )(*arrays, *after)


LOW, HIGH = slice(0, 2), slice(2, 4)


def _sums_kernel(terms, *refs):
    outs = refs[len(refs) - len(terms) :]
    for out, pairs in zip(outs, terms):
        total = refs[pairs[0][0]][:, pairs[0][1]]
        for i, part in pairs[1:]:
            total = total + refs[i][:, part]
        out[...] = total


def _sums(inputs, terms, name, after=()):
    return pl.pallas_call(
        functools.partial(_sums_kernel, terms),
        in_specs=[pl.BlockSpec()] * len(inputs) + [pl.BlockSpec(memory_space=pl.ANY)] * len(after),
        out_shape=[_shape(2, 2, 8, 4096)] * len(terms),
        compiler_params=_params(),
        cost_estimate=COST,
        name=name,
    )(*inputs, *after)


def _second_kernel(low, high, got, low1, high3, *outs):
    core, x, y, _, _, _ = _position()
    for k in range(4):
        i = (y + k) % 4

        @pl.when((core == 0) & (i < 2))
        def _():
            total = (low[:, i] + got[:, i]) + low1[:, i]
            for j in range(4):
                outs[k][:, j] = total[:, :, j * 1024 : (j + 1) * 1024]

        @pl.when((core == 0) & (i >= 2))
        def _():
            total = (high[:, i - 2] + got[:, i]) + high3[:, i - 2]
            for j in range(4):
                outs[k][:, j] = total[:, :, j * 1024 : (j + 1) * 1024]

        @pl.when(core == 1)
        def _():
            at = pl.ds(pl.multiple_of(((x + k) % 4) * 1024, 1024), 1024)
            for j in range(2):
                outs[k][:, j] = (low[:, j, :, at] + got[:, j, :, at]) + low1[:, j, :, at]
                outs[k][:, j + 2] = (high[:, j, :, at] + got[:, j + 2, :, at]) + high3[:, j, :, at]


def _second(*parts):
    return pl.pallas_call(
        _second_kernel, out_shape=[_shape(2, 4, 8, 1024)] * 4, compiler_params=_params(), cost_estimate=COST, name="first_axis_sum"
    )(*parts)


def _third_kernel(a, b, c, d, out):
    out[...] = (a[...] + b[...]) + (c[...] + d[...])


def _third(parts):
    return pl.pallas_call(
        _third_kernel, out_shape=_shape(2, 4, 8, 1024), compiler_params=_params(), cost_estimate=COST, name="second_axis_sum"
    )(*parts)


def _mean_kernel(a, b, c, d, out, means):
    core, _, _, z, _, _ = _position()
    lines = []
    for j in range(4):
        total = (a[0, j] + b[0, j]) + (c[0, j] + d[0, j])
        count = (a[1, j] + b[1, j]) + (c[1, j] + d[1, j])
        means[j] = total / (count + 1.0)
        lines += [jnp.sum(means[j, 0:4], axis=0, keepdims=True), jnp.sum(means[j, 4:8], axis=0, keepdims=True)]
    four = jnp.concatenate(lines, axis=0)
    row = lax.broadcasted_iota(jnp.int32, (512, 128), 0)
    column = lax.broadcasted_iota(jnp.int32, (512, 128), 1)
    pool = jnp.where(row // 4 == column, 0.0625, 0.0).astype(F32)
    for j in range(4):
        out[:, j * 1024 : (j + 1) * 1024] = means[jnp.where(core == 0, j, z ^ j)]
    for j in range(2):
        out[:, 4096 + j * 128 : 4096 + (j + 1) * 128] = jnp.dot(
            four[:, j * 512 : (j + 1) * 512], pool, precision=lax.Precision.HIGHEST, preferred_element_type=F32
        )


def _mean(parts):
    return pl.pallas_call(
        _mean_kernel,
        out_shape=_shape(8, 4352),
        scratch_shapes=[pltpu.VMEM((4, 8, 1024), F32)],
        compiler_params=_params(),
        cost_estimate=COST,
        name="mean_and_preview",
    )(*parts)


def _row_kernel(a, b, c, d, out):
    for k, part in enumerate((a, b, c, d)):
        out[k, :, :1024] = part[:, :1024]
        out[k, :, 1024:] = part[:, 4096:]


def _row(parts):
    return pl.pallas_call(
        _row_kernel, out_shape=_shape(4, 8, 1280), compiler_params=_params(), cost_estimate=COST, name="gathered_row"
    )(*parts)


def _final_kernel(*refs):
    own_rows, other_rows, own, other = (refs[4 * i : 4 * i + 4] for i in range(4))
    grid, preview, lines = refs[16:]
    me, x, y, z, _, _ = _position()

    def place(rows0, last0, last1):
        for k in range(4):
            fy, fz = y ^ k, z ^ k
            grid[pl.ds(pl.multiple_of(fy * 8, 8), 8), :] = rows0[k][:, :4096]
            for i in range(4):
                for j in range(4):
                    lines[fz * 8 + (y ^ i), :, j * 256 : (j + 1) * 256] = last0[k][i, 2 * j : 2 * j + 2, 1024:]
            for i in range(4):
                fx = x ^ i
                columns = pl.ds(pl.multiple_of(fx * 1024, 1024), 1024)
                grid[pl.ds(pl.multiple_of(32 + fy * 8, 8), 8), columns] = last1[k][i, :, :1024]
                at = pl.ds(pl.multiple_of(fx * 256, 256), 256)
                for j in range(4):
                    lines[j * 8 + 4 + fy, :, at] = last1[k][i, 2 * j : 2 * j + 2, 1024:]

    @pl.when(me == 0)
    def _():
        place(own_rows, own, other)

    @pl.when(me == 1)
    def _():
        place(other_rows, other, own)

    for i in range(8):
        preview[8 * i : 8 * i + 8, :] = jnp.concatenate([lines[4 * i + j] for j in range(4)], axis=0)


def _final(own_rows, other_rows, own, other):
    return pl.pallas_call(
        _final_kernel,
        out_shape=[_shape(64, 4096), _shape(64, 1024)],
        scratch_shapes=[pltpu.VMEM((32, 2, 1024), F32)],
        compiler_params=_params(),
        cost_estimate=COST,
        name="assemble",
    )(*own_rows, *other_rows, *own, *other)


def _first_axis(arrays):
    near, far = _partner(1, Z, Y), _partner(3, Z, Y)
    whole = slice(None)
    sent2, own2 = _blocks(arrays, ((2, False), (2, True)))
    got2 = _send(sent2, _SIBLING)
    sent1, sent3 = _blocks(arrays, ((1, False), (3, False)), (own2,))
    got1, got3 = _send(sent1, _SIBLING), _send(sent3, _SIBLING)
    low2, high2 = _sums((own2, got2), [[(0, LOW), (1, LOW)], [(0, HIGH), (1, HIGH)]], "opposite_pair", (sent1,))
    low, high = _send(low2, near), _send(high2, far)
    own1, own3, sent0, own0 = _blocks(arrays, ((1, True), (3, True), (0, False), (0, True)), (low2,))
    low1, high1, low3, high3 = _sums(
        (own1, got1, own3, got3),
        [[(0, LOW), (1, LOW)], [(0, HIGH), (1, HIGH)], [(2, LOW), (3, LOW)], [(2, HIGH), (3, HIGH)]],
        "neighbour_pairs",
    )
    got0 = _send(sent0, _SIBLING)
    low1, high3 = _send(low1, near), _send(high3, far)
    low3, high1 = _sums((low3, low, high1, high), [[(0, whole), (1, whole)], [(2, whole), (3, whole)]], "passed_on")
    low, high = _sums(
        (own0, low1, high3),
        [[(0, LOW), (1, whole)], [(0, HIGH), (2, whole)]],
        "early_sum",
    )
    return _second(low, high, got0, _send(low3, far), _send(high1, near))


def _local(p, c, n):
    arrays = [pltpu.with_memory_space_constraint(array, pltpu.HBM) for array in (p, c, n)]
    both = _third(_exchange(_first_axis(arrays), Y, X, _shift))
    packed = _mean(_exchange([both] * 4, X, Z))
    rows = _exchange([packed] * 4, Y, X)
    last = _exchange([_row(rows)] * 4, Z, Y)
    return _final(rows, [_send(part, _SIBLING) for part in rows], last, [_send(part, _SIBLING) for part in last])


def solution(mesh):
    return jax.shard_map(
        _local,
        mesh=mesh,
        in_specs=(P(AXES, None, None),) * 3,
        out_specs=(P("gz", None), P(None, None)),
        check_vma=False,
    )
```

```python
import functools

import jax
import jax.numpy as jnp
import numpy as np
from jax import lax
from jax.experimental import pallas as pl
from jax.experimental.pallas import tpu as pltpu
from jax.sharding import PartitionSpec as P

AXES = ("gx", "gy", "gz")
F32 = jnp.float32
COST = pl.CostEstimate(flops=1, bytes_accessed=1, transcendentals=0)
VMEM_LIMIT = 20 * 1024 * 1024


def _coords(d):
    gx, gy, gz = d // 32, (d // 4) % 8, d % 4
    return (gx // 2) * 2 + gy % 2, gy // 2, gz, gx % 2


def _device(x, y, z, core):
    return ((x // 2) * 2 + core) * 32 + (y * 2 + x % 2) * 4 + z


X, Y, Z = 0, 1, 2


X, Y, Z = 0, 1, 2


_SIBLING = [(d, d ^ 32) for d in range(128)]


def _send(array, pairs):
    return lax.ppermute(array, AXES, pairs)


def _partner(k, axis0, axis1):
    pairs = []
    for d in range(128):
        at = list(_coords(d))
        at[(axis0, axis1)[at[3]]] ^= k
        pairs.append((d, _device(*at)))
    return pairs


SECOND, THIRD, ROWS, LAST = (0, 2, 3, 1), (0, 1, 2, 3), (0, 1, 2, 3), (0, 1, 3, 2)


def _exchange(arrays, axis0, axis1, places):
    return [arrays[0]] + [_send(arrays[k], _partner(places[k], axis0, axis1)) for k in (1, 2, 3)]


def _position():
    gx, gy, gz = (lax.axis_index(a) for a in AXES)
    core = gx % 2
    x, y = (gx // 2) * 2 + gy % 2, gy // 2
    first, second = jnp.where(core == 0, gz, y), jnp.where(core == 0, y, gz)
    return core, x, y, gz, first, second


def _shape(*dims):
    return jax.ShapeDtypeStruct(dims, F32)


def _params():
    return pltpu.CompilerParams(vmem_limit_bytes=VMEM_LIMIT)


def _blocks_kernel(wanted, *refs):
    p, c, n = refs[:3]
    outs, held, sems = refs[-2 - len(wanted) : -2], refs[-2], refs[-1]
    me, _, y, z, _, _ = _position()
    copies = []
    for j, (k, own) in enumerate(wanted):
        core = me if own else 1 - me
        a = jnp.where(core == 0, z, y) ^ k
        for b in range(4):
            rows = pl.ds(pl.multiple_of(jnp.where(core == 0, a * 8 + b, b * 8 + 4 + a) * 8, 8), 8)
            for i, array in enumerate((p, c, n)):
                copy = pltpu.make_async_copy(array.at[0, rows], held.at[i, j, b], sems.at[i, j, b])
                copy.start()
                copies.append((i, j, b, copy))
    for i, j, b, copy in copies:
        copy.wait()
        if i == 2:
            outs[j][0, b] = held[0, j, b] + held[1, j, b]
            outs[j][1, b] = held[2, j, b]


def _blocks(arrays, wanted, after=()):
    return pl.pallas_call(
        functools.partial(_blocks_kernel, wanted),
        in_specs=[pl.BlockSpec(memory_space=pltpu.HBM)] * 3 + [pl.BlockSpec(memory_space=pl.ANY)] * len(after),
        out_shape=[_shape(2, 4, 8, 4096)] * len(wanted),
        scratch_shapes=[pltpu.VMEM((3, len(wanted), 4, 8, 4096), F32), pltpu.SemaphoreType.DMA((3, len(wanted), 4))],
        compiler_params=_params(),
        cost_estimate=COST,
        name="local_blocks",
    )(*arrays, *after)


LOW, HIGH = slice(0, 2), slice(2, 4)


def _sums_kernel(terms, *refs):
    outs = refs[len(refs) - len(terms) :]
    for out, pairs in zip(outs, terms):
        total = refs[pairs[0][0]][:, pairs[0][1]]
        for i, part in pairs[1:]:
            total = total + refs[i][:, part]
        out[...] = total


def _sums(inputs, terms, name, after=()):
    return pl.pallas_call(
        functools.partial(_sums_kernel, terms),
        in_specs=[pl.BlockSpec()] * len(inputs) + [pl.BlockSpec(memory_space=pl.ANY)] * len(after),
        out_shape=[_shape(2, 2, 8, 4096)] * len(terms),
        compiler_params=_params(),
        cost_estimate=COST,
        name=name,
    )(*inputs, *after)


def _second_kernel(low, high, got, low1, high3, *outs):
    core, x, y, _, _, _ = _position()
    for k in range(4):
        i = y ^ SECOND[k]

        @pl.when((core == 0) & (i < 2))
        def _():
            total = (low[:, i] + got[:, i]) + low1[:, i]
            for j in range(4):
                outs[k][:, j] = total[:, :, j * 1024 : (j + 1) * 1024]

        @pl.when((core == 0) & (i >= 2))
        def _():
            total = (high[:, i - 2] + got[:, i]) + high3[:, i - 2]
            for j in range(4):
                outs[k][:, j] = total[:, :, j * 1024 : (j + 1) * 1024]

        @pl.when(core == 1)
        def _():
            at = pl.ds(pl.multiple_of((x ^ SECOND[k]) * 1024, 1024), 1024)
            for j in range(2):
                outs[k][:, j] = (low[:, j, :, at] + got[:, j, :, at]) + low1[:, j, :, at]
                outs[k][:, j + 2] = (high[:, j, :, at] + got[:, j + 2, :, at]) + high3[:, j, :, at]


def _second(*parts):
    return pl.pallas_call(
        _second_kernel, out_shape=[_shape(2, 4, 8, 1024)] * 4, compiler_params=_params(), cost_estimate=COST, name="first_axis_sum"
    )(*parts)


def _third_kernel(a, b, c, d, out):
    out[...] = (a[...] + b[...]) + (c[...] + d[...])


def _third(parts):
    return pl.pallas_call(
        _third_kernel, out_shape=_shape(2, 4, 8, 1024), compiler_params=_params(), cost_estimate=COST, name="second_axis_sum"
    )(*parts)


def _mean_kernel(a, b, c, d, out, means):
    core, _, _, z, _, _ = _position()
    lines = []
    for j in range(4):
        total = (a[0, j] + b[0, j]) + (c[0, j] + d[0, j])
        count = (a[1, j] + b[1, j]) + (c[1, j] + d[1, j])
        means[j] = total / (count + 1.0)
        lines += [jnp.sum(means[j, 0:4], axis=0, keepdims=True), jnp.sum(means[j, 4:8], axis=0, keepdims=True)]
    four = jnp.concatenate(lines, axis=0)
    row = lax.broadcasted_iota(jnp.int32, (512, 128), 0)
    column = lax.broadcasted_iota(jnp.int32, (512, 128), 1)
    pool = jnp.where(row // 4 == column, 0.0625, 0.0).astype(F32)
    for j in range(4):
        out[:, j * 1024 : (j + 1) * 1024] = means[jnp.where(core == 0, j, z ^ j)]
    for j in range(2):
        out[:, 4096 + j * 128 : 4096 + (j + 1) * 128] = jnp.dot(
            four[:, j * 512 : (j + 1) * 512], pool, precision=lax.Precision.HIGHEST, preferred_element_type=F32
        )


def _mean(parts):
    return pl.pallas_call(
        _mean_kernel,
        out_shape=_shape(8, 4352),
        scratch_shapes=[pltpu.VMEM((4, 8, 1024), F32)],
        compiler_params=_params(),
        cost_estimate=COST,
        name="mean_and_preview",
    )(*parts)


def _row_kernel(a, b, c, d, out, whole):
    for k, part in enumerate((a, b, c, d)):
        out[k, :, :1024] = part[:, :1024]
        out[k, :, 1024:] = part[:, 4096:]
        whole[k] = part[...]


def _row(parts):
    return pl.pallas_call(
        _row_kernel,
        out_shape=[_shape(4, 8, 1280), _shape(4, 8, 4352)],
        compiler_params=_params(),
        cost_estimate=COST,
        name="gathered_row",
    )(*parts)


def _final_kernel(own_rows, other_rows, *refs):
    own, other, (grid, preview, lines) = refs[:3], refs[3:6], refs[6:]
    me, x, y, z, _, _ = _position()

    def place(rows0, last0, rows1, last1):
        for k in range(4):
            grid[pl.ds(pl.multiple_of((y ^ ROWS[k]) * 8, 8), 8), :] = rows0[k, :, :4096]
            fz, fy = z ^ LAST[k], y ^ LAST[k]
            for i in range(4):
                for j in range(4):
                    two = slice(2 * j, 2 * j + 2)
                    line = rows0[i, two, 4096:] if k == 0 else last0[k - 1][i, two, 1024:]
                    lines[fz * 8 + (y ^ ROWS[i]), :, j * 256 : (j + 1) * 256] = line
            for i in range(4):
                fx = x ^ ROWS[i]
                columns = pl.ds(pl.multiple_of(fx * 1024, 1024), 1024)
                block = rows1[i, :, :1024] if k == 0 else last1[k - 1][i, :, :1024]
                grid[pl.ds(pl.multiple_of(32 + fy * 8, 8), 8), columns] = block
                at = pl.ds(pl.multiple_of(fx * 256, 256), 256)
                for j in range(4):
                    two = slice(2 * j, 2 * j + 2)
                    line = rows1[i, two, 4096:] if k == 0 else last1[k - 1][i, two, 1024:]
                    lines[j * 8 + 4 + fy, :, at] = line

    @pl.when(me == 0)
    def _():
        place(own_rows, own, other_rows, other)

    @pl.when(me == 1)
    def _():
        place(other_rows, other, own_rows, own)

    for i in range(8):
        preview[8 * i : 8 * i + 8, :] = jnp.concatenate([lines[4 * i + j] for j in range(4)], axis=0)


def _final(own_rows, other_rows, own, other):
    return pl.pallas_call(
        _final_kernel,
        out_shape=[_shape(64, 4096), _shape(64, 1024)],
        scratch_shapes=[pltpu.VMEM((32, 2, 1024), F32)],
        compiler_params=_params(),
        cost_estimate=COST,
        name="assemble",
    )(own_rows, other_rows, *own, *other)


def _first_axis(arrays):
    near, far = _partner(1, Z, Y), _partner(3, Z, Y)
    whole = slice(None)
    sent2, own2 = _blocks(arrays, ((2, False), (2, True)))
    got2 = _send(sent2, _SIBLING)
    sent1, sent3 = _blocks(arrays, ((1, False), (3, False)), (own2,))
    got1, got3 = _send(sent1, _SIBLING), _send(sent3, _SIBLING)
    low2, high2 = _sums((own2, got2), [[(0, LOW), (1, LOW)], [(0, HIGH), (1, HIGH)]], "opposite_pair", (sent1,))
    low, high = _send(low2, near), _send(high2, far)
    own1, own3, sent0, own0 = _blocks(arrays, ((1, True), (3, True), (0, False), (0, True)), (low2,))
    low1, high1, low3, high3 = _sums(
        (own1, got1, own3, got3),
        [[(0, LOW), (1, LOW)], [(0, HIGH), (1, HIGH)], [(2, LOW), (3, LOW)], [(2, HIGH), (3, HIGH)]],
        "neighbour_pairs",
    )
    got0 = _send(sent0, _SIBLING)
    low1, high3 = _send(low1, near), _send(high3, far)
    low3, high1 = _sums((low3, low, high1, high), [[(0, whole), (1, whole)], [(2, whole), (3, whole)]], "passed_on")
    low, high = _sums(
        (own0, low1, high3),
        [[(0, LOW), (1, whole)], [(0, HIGH), (2, whole)]],
        "early_sum",
    )
    return _second(low, high, got0, _send(low3, far), _send(high1, near))


def _local(p, c, n):
    arrays = [pltpu.with_memory_space_constraint(array, pltpu.HBM) for array in (p, c, n)]
    both = _third(_exchange(_first_axis(arrays), Y, X, SECOND))
    packed = _mean(_exchange([both] * 4, X, Z, THIRD))
    row, rows = _row(_exchange([packed] * 4, Y, X, ROWS))
    last = _exchange([row] * 4, Z, Y, LAST)[1:]
    return _final(rows, _send(rows, _SIBLING), last, [_send(part, _SIBLING) for part in last])


def solution(mesh):
    return jax.shard_map(
        _local,
        mesh=mesh,
        in_specs=(P(AXES, None, None),) * 3,
        out_specs=(P("gz", None), P(None, None)),
        check_vma=False,
    )
```

```python
import functools

import jax
import jax.numpy as jnp
import numpy as np
from jax import lax
from jax.experimental import pallas as pl
from jax.experimental.pallas import tpu as pltpu
from jax.sharding import PartitionSpec as P

AXES = ("gx", "gy", "gz")
F32 = jnp.float32
COST = pl.CostEstimate(flops=1, bytes_accessed=1, transcendentals=0)
VMEM_LIMIT = 20 * 1024 * 1024


def _coords(d):
    gx, gy, gz = d // 32, (d // 4) % 8, d % 4
    return (gx // 2) * 2 + gy % 2, gy // 2, gz, gx % 2


def _device(x, y, z, core):
    return ((x // 2) * 2 + core) * 32 + (y * 2 + x % 2) * 4 + z


X, Y, Z = 0, 1, 2


X, Y, Z = 0, 1, 2


_SIBLING = [(d, d ^ 32) for d in range(128)]


def _send(array, pairs):
    return lax.ppermute(array, AXES, pairs)


def _partner(k, axis0, axis1):
    pairs = []
    for d in range(128):
        at = list(_coords(d))
        at[(axis0, axis1)[at[3]]] ^= k
        pairs.append((d, _device(*at)))
    return pairs


SECOND, THIRD, ROWS, LAST = (0, 2, 3, 1), (0, 1, 2, 3), (0, 1, 2, 3), (0, 1, 3, 2)


def _exchange(arrays, axis0, axis1, places):
    return [arrays[0]] + [_send(arrays[k], _partner(places[k], axis0, axis1)) for k in (1, 2, 3)]


def _position():
    gx, gy, gz = (lax.axis_index(a) for a in AXES)
    core = gx % 2
    x, y = (gx // 2) * 2 + gy % 2, gy // 2
    first, second = jnp.where(core == 0, gz, y), jnp.where(core == 0, y, gz)
    return core, x, y, gz, first, second


def _shape(*dims):
    return jax.ShapeDtypeStruct(dims, F32)


def _params():
    return pltpu.CompilerParams(vmem_limit_bytes=VMEM_LIMIT)


def _blocks_kernel(wanted, *refs):
    p, c, n = refs[:3]
    outs, held, sems = refs[-2 - len(wanted) : -2], refs[-2], refs[-1]
    me, _, y, z, _, _ = _position()
    copies = []
    for j, (k, own) in enumerate(wanted):
        core = me if own else 1 - me
        a = jnp.where(core == 0, z, y) ^ k
        for b in range(4):
            rows = pl.ds(pl.multiple_of(jnp.where(core == 0, a * 8 + b, b * 8 + 4 + a) * 8, 8), 8)
            for i, array in enumerate((p, c, n)):
                copy = pltpu.make_async_copy(array.at[0, rows], held.at[i, j, b], sems.at[i, j, b])
                copy.start()
                copies.append((i, j, b, copy))
    for i, j, b, copy in copies:
        copy.wait()
        if i == 2:
            outs[j][0, b] = held[0, j, b] + held[1, j, b]
            outs[j][1, b] = held[2, j, b]


def _blocks(arrays, wanted, after=()):
    return pl.pallas_call(
        functools.partial(_blocks_kernel, wanted),
        in_specs=[pl.BlockSpec(memory_space=pltpu.HBM)] * 3 + [pl.BlockSpec(memory_space=pl.ANY)] * len(after),
        out_shape=[_shape(2, 4, 8, 4096)] * len(wanted),
        scratch_shapes=[pltpu.VMEM((3, len(wanted), 4, 8, 4096), F32), pltpu.SemaphoreType.DMA((3, len(wanted), 4))],
        compiler_params=_params(),
        cost_estimate=COST,
        name="local_blocks",
    )(*arrays, *after)


LOW, HIGH = slice(0, 2), slice(2, 4)


def _sums_kernel(terms, *refs):
    outs = refs[len(refs) - len(terms) :]
    for out, pairs in zip(outs, terms):
        total = refs[pairs[0][0]][:, pairs[0][1]]
        for i, part in pairs[1:]:
            total = total + refs[i][:, part]
        out[...] = total


def _sums(inputs, terms, name, after=()):
    return pl.pallas_call(
        functools.partial(_sums_kernel, terms),
        in_specs=[pl.BlockSpec()] * len(inputs) + [pl.BlockSpec(memory_space=pl.ANY)] * len(after),
        out_shape=[_shape(2, 2, 8, 4096)] * len(terms),
        compiler_params=_params(),
        cost_estimate=COST,
        name=name,
    )(*inputs, *after)


def _second_kernel(low, high, got, low1, high3, *outs):
    core, x, y, _, _, _ = _position()
    for k in range(4):
        i = y ^ SECOND[k]

        @pl.when((core == 0) & (i < 2))
        def _():
            total = (low[:, i] + got[:, i]) + low1[:, i]
            for j in range(4):
                outs[k][:, j] = total[:, :, j * 1024 : (j + 1) * 1024]

        @pl.when((core == 0) & (i >= 2))
        def _():
            total = (high[:, i - 2] + got[:, i]) + high3[:, i - 2]
            for j in range(4):
                outs[k][:, j] = total[:, :, j * 1024 : (j + 1) * 1024]

        @pl.when(core == 1)
        def _():
            at = pl.ds(pl.multiple_of((x ^ SECOND[k]) * 1024, 1024), 1024)
            for j in range(2):
                outs[k][:, j] = (low[:, j, :, at] + got[:, j, :, at]) + low1[:, j, :, at]
                outs[k][:, j + 2] = (high[:, j, :, at] + got[:, j + 2, :, at]) + high3[:, j, :, at]


def _second(*parts):
    return pl.pallas_call(
        _second_kernel, out_shape=[_shape(2, 4, 8, 1024)] * 4, compiler_params=_params(), cost_estimate=COST, name="first_axis_sum"
    )(*parts)


def _third_kernel(a, b, c, d, out):
    out[...] = (a[...] + b[...]) + (c[...] + d[...])


def _third(parts):
    return pl.pallas_call(
        _third_kernel, out_shape=_shape(2, 4, 8, 1024), compiler_params=_params(), cost_estimate=COST, name="second_axis_sum"
    )(*parts)


def _mean_kernel(a, b, c, d, out, means):
    core, _, _, z, _, _ = _position()
    lines = []
    for j in range(4):
        total = (a[0, j] + b[0, j]) + (c[0, j] + d[0, j])
        count = (a[1, j] + b[1, j]) + (c[1, j] + d[1, j])
        means[j] = total / (count + 1.0)
        lines += [jnp.sum(means[j, 0:4], axis=0, keepdims=True), jnp.sum(means[j, 4:8], axis=0, keepdims=True)]
    four = jnp.concatenate(lines, axis=0)
    row = lax.broadcasted_iota(jnp.int32, (512, 128), 0)
    column = lax.broadcasted_iota(jnp.int32, (512, 128), 1)
    pool = jnp.where(row // 4 == column, 0.0625, 0.0).astype(F32)
    for j in range(4):
        out[:, j * 1024 : (j + 1) * 1024] = means[jnp.where(core == 0, j, z ^ j)]
    for j in range(2):
        out[:, 4096 + j * 128 : 4096 + (j + 1) * 128] = jnp.dot(
            four[:, j * 512 : (j + 1) * 512], pool, precision=lax.Precision.HIGHEST, preferred_element_type=F32
        )


def _mean(parts):
    return pl.pallas_call(
        _mean_kernel,
        out_shape=_shape(8, 4352),
        scratch_shapes=[pltpu.VMEM((4, 8, 1024), F32)],
        compiler_params=_params(),
        cost_estimate=COST,
        name="mean_and_preview",
    )(*parts)


def _row_kernel(a, b, c, d, out, whole):
    for k, part in enumerate((a, b, c, d)):
        out[k, :, :1024] = part[:, :1024]
        out[k, :, 1024:] = part[:, 4096:]
        whole[k] = part[...]


def _row(parts):
    return pl.pallas_call(
        _row_kernel,
        out_shape=[_shape(4, 8, 1280), _shape(4, 8, 4352)],
        compiler_params=_params(),
        cost_estimate=COST,
        name="gathered_row",
    )(*parts)


def _final_kernel(own_rows, other_rows, *refs):
    own, other, (grid, preview, lines) = refs[:3], refs[3:6], refs[6:]
    me, x, y, z, _, _ = _position()

    def place(rows0, last0, rows1, last1):
        for k in range(4):
            grid[pl.ds(pl.multiple_of((y ^ ROWS[k]) * 8, 8), 8), :] = rows0[k, :, :4096]
            fz, fy = z ^ LAST[k], y ^ LAST[k]
            for i in range(4):
                for j in range(4):
                    two = slice(2 * j, 2 * j + 2)
                    line = rows0[i, two, 4096:] if k == 0 else last0[k - 1][i, two, 1024:]
                    lines[fz * 8 + (y ^ ROWS[i]), :, j * 256 : (j + 1) * 256] = line
            for i in range(4):
                fx = x ^ ROWS[i]
                columns = pl.ds(pl.multiple_of(fx * 1024, 1024), 1024)
                block = rows1[i, :, :1024] if k == 0 else last1[k - 1][i, :, :1024]
                grid[pl.ds(pl.multiple_of(32 + fy * 8, 8), 8), columns] = block
                at = pl.ds(pl.multiple_of(fx * 256, 256), 256)
                for j in range(4):
                    two = slice(2 * j, 2 * j + 2)
                    line = rows1[i, two, 4096:] if k == 0 else last1[k - 1][i, two, 1024:]
                    lines[j * 8 + 4 + fy, :, at] = line

    @pl.when(me == 0)
    def _():
        place(own_rows, own, other_rows, other)

    @pl.when(me == 1)
    def _():
        place(other_rows, other, own_rows, own)

    for i in range(8):
        preview[8 * i : 8 * i + 8, :] = jnp.concatenate([lines[4 * i + j] for j in range(4)], axis=0)


def _final(own_rows, other_rows, own, other):
    return pl.pallas_call(
        _final_kernel,
        out_shape=[_shape(64, 4096), _shape(64, 1024)],
        scratch_shapes=[pltpu.VMEM((32, 2, 1024), F32)],
        compiler_params=_params(),
        cost_estimate=COST,
        name="assemble",
    )(own_rows, other_rows, *own, *other)


def _first_axis(arrays):
    near, far = _partner(3, Z, Y), _partner(1, Z, Y)
    whole = slice(None)
    sent2, own2 = _blocks(arrays, ((2, False), (2, True)))
    got2 = _send(sent2, _SIBLING)
    sent_near, sent_far = _blocks(arrays, ((3, False), (1, False)), (own2,))
    got_near, got_far = _send(sent_near, _SIBLING), _send(sent_far, _SIBLING)
    low2, high2 = _sums((own2, got2), [[(0, LOW), (1, LOW)], [(0, HIGH), (1, HIGH)]], "opposite_pair", (sent_near,))
    low, high = _send(low2, near), _send(high2, far)
    own_near, own_far, sent0, own0 = _blocks(arrays, ((3, True), (1, True), (0, False), (0, True)), (low2,))
    low_near, high_near, low_far, high_far = _sums(
        (own_near, got_near, own_far, got_far),
        [[(0, LOW), (1, LOW)], [(0, HIGH), (1, HIGH)], [(2, LOW), (3, LOW)], [(2, HIGH), (3, HIGH)]],
        "neighbour_pairs",
    )
    got0 = _send(sent0, _SIBLING)
    low_near, high_far = _send(low_near, near), _send(high_far, far)
    low_far, high_near = _sums((low_far, low, high_near, high), [[(0, whole), (1, whole)], [(2, whole), (3, whole)]], "passed_on")
    low, high = _sums(
        (own0, low_near, high_far),
        [[(0, LOW), (1, whole)], [(0, HIGH), (2, whole)]],
        "early_sum",
    )
    return _second(low, high, got0, _send(low_far, far), _send(high_near, near))


def _local(p, c, n):
    arrays = [pltpu.with_memory_space_constraint(array, pltpu.HBM) for array in (p, c, n)]
    both = _third(_exchange(_first_axis(arrays), Y, X, SECOND))
    packed = _mean(_exchange([both] * 4, X, Z, THIRD))
    row, rows = _row(_exchange([packed] * 4, Y, X, ROWS))
    last = _exchange([row] * 4, Z, Y, LAST)[1:]
    return _final(rows, _send(rows, _SIBLING), last, [_send(part, _SIBLING) for part in last])


def solution(mesh):
    return jax.shard_map(
        _local,
        mesh=mesh,
        in_specs=(P(AXES, None, None),) * 3,
        out_specs=(P("gz", None), P(None, None)),
        check_vma=False,
    )
```
